32 devices in a mesh: groups: 2 (over x), rows: 16 (over z, y, core).
Axes of the slice: x: 2, y: 2, z: 4, core: 2. Of those that a mesh axis runs over, the one named last changes fastest.
Arguments:
- hamiltonian: bfloat16 [1536, 64, 1920], P(('groups', 'rows')), parts along dimension 0, may hold values from -0.125 to 0.125
- column_blocks: int32 [1536, 30], P(('groups', 'rows')), parts along dimension 0, may hold values from 0 to 767, as said below
- block_counts: int32 [1536], P(('groups', 'rows')), parts along dimension 0, may hold values from 1 to 30, as said below
- trial_vectors: bfloat16 [1536, 64, 128], P(('groups', 'rows')), parts along dimension 0, may hold values from -6 to 6
- spectral_bounds: float32 [4], P('groups'), parts along dimension 0, may hold values from -1.6 to 1.6, as said below
Outputs:
- filtered: bfloat16 [1536, 64, 128], P(('groups', 'rows')), parts along dimension 0
The draws below stay inside these ranges and needn't reach their ends.
There are 2 independent parts, one for each index of `groups`. The reference program is written for one: setup_inputs(seed, part) draws one part's arguments, and reference() takes and returns one part's arrays. A program takes and returns all parts, laid end to end along the dimension named above; each array names one. Nothing has to cross between parts.
Inputs may be any that keep to these rules, and one draw needn't show every extreme that they name: column_blocks[r, j] = (r + o) mod 768 where the offsets o of one row are distinct and lie in -16 to 16; offsets of both ends occur. `block_counts`: some row uses all slots and some row uses one. `spectral_bounds`: lower end below -0.9, upper end above 0.9.
All inputs are finite; a program needn't handle non-finite values.
Results may differ from the reference program's by a relative error of at most 0.0041.
Values may be sent and summed in bfloat16 or wider, within the bound.
A program may use at most 256 MiB of HBM per device.

```python
import jax
import jax.numpy as jnp
from jax import lax

B = 64
K = 128
NZ = 30
REACH = 16
RB_DEV = 48
NB = 768


def draw_column_blocks(key, part):
    key = jax.random.fold_in(key, 2)
    choices_total = 2 * REACH + 1
    scores = jax.random.randint(key, (NB, choices_total), 0, 2 ** 20)
    scores = scores * choices_total + jnp.arange(choices_total, dtype=jnp.int32)[None, :]
    order = jnp.argsort(scores, axis=1)[:, :NZ].astype(jnp.int32)
    offsets = order - REACH
    row_ids = jnp.arange(NB, dtype=jnp.int32)[:, None]
    return ((row_ids + offsets + NB) % NB).astype(jnp.int32)


def draw_block_counts(key, part):
    key = jax.random.fold_in(key, 1)
    key_counts, key_full, key_single = jax.random.split(key, 3)
    counts = jax.random.randint(key_counts, (NB,), 1, NZ + 1)
    full_row = jax.random.randint(key_full, (), 0, NB)
    single_row = (full_row + 1 + jax.random.randint(key_single, (), 0, NB - 1)) % NB
    counts = counts.at[full_row].set(NZ)
    counts = counts.at[single_row].set(1)
    return counts.astype(jnp.int32)


def draw_spectral_bounds(key, part):
    key = jax.random.fold_in(key, 3)
    key_lower, key_upper = jax.random.split(key)
    lower_end = jax.random.uniform(key_lower, (1,), jnp.float32, -1.6, -0.9)
    upper_end = jax.random.uniform(key_upper, (1,), jnp.float32, 0.9, 1.6)
    return jnp.concatenate([lower_end, upper_end]).astype(jnp.float32)


def steps_of(key, shape, shards, low, high):
    def one(axis_at, shards_of):
        heights = jax.random.uniform(jax.random.fold_in(jax.random.fold_in(key, 6), axis_at), (shards_of,), jnp.float32, low / len(shards), high / len(shards))
        return jnp.repeat(jnp.exp(heights), shape[axis_at] // shards_of).reshape((-1,) + (1,) * (len(shape) - axis_at - 1))

    loudness = one(*shards[0])
    for cut in shards[1:]:
        loudness = loudness * one(*cut)
    return loudness


def gaussian(key, shape, spread, limit, shards=(), kind=jnp.bfloat16):
    values = spread * jax.random.normal(key, shape, jnp.float32)
    if shards:
        values = values * steps_of(key, shape, shards, -0.22, 0.18)
    return jnp.clip(values, -limit, limit).astype(kind)


def setup_inputs(seed: int = 0, part: int = 0) -> dict:
    arg_keys = jax.random.split(jax.random.key(seed), 6)
    part_keys = jax.random.split(jax.random.fold_in(arg_keys[5], part), 6)
    hamiltonian = gaussian(part_keys[0], (NB, B, NZ * B), (NZ * B) ** -0.5, 0.125, ((0, 16),))
    column_blocks = draw_column_blocks(jax.random.fold_in(jax.random.fold_in(arg_keys[5], part), 71), part)
    block_counts = draw_block_counts(jax.random.fold_in(jax.random.fold_in(arg_keys[5], part), 71), part)
    trial_vectors = gaussian(part_keys[3], (NB, B, K), 1.0, 6.0, ((0, 16),))
    spectral_bounds = draw_spectral_bounds(jax.random.fold_in(jax.random.fold_in(arg_keys[5], part), 71), part)
    return dict(hamiltonian=hamiltonian, column_blocks=column_blocks, block_counts=block_counts, trial_vectors=trial_vectors, spectral_bounds=spectral_bounds)


def apply_blocks(panels, hamiltonian, column_blocks, block_counts):
    group_total = NB // RB_DEV

    def one_group(group_index):
        offset_row = (group_index * RB_DEV).astype(jnp.int32)
        ham_rows = lax.dynamic_slice_in_dim(hamiltonian, offset_row, RB_DEV, 0).astype(jnp.float32)
        index_rows = lax.dynamic_slice_in_dim(column_blocks, offset_row, RB_DEV, 0)
        count_rows = lax.dynamic_slice_in_dim(block_counts, offset_row, RB_DEV, 0)
        gathered = panels[index_rows].astype(jnp.float32)
        valid_slot = jnp.arange(NZ, dtype=jnp.int32)[None, :] < count_rows[:, None]
        gathered = jnp.where(valid_slot[:, :, None, None], gathered, jnp.float32(0.0))
        gathered = gathered.reshape(RB_DEV, NZ * B, K)
        return jnp.einsum('rak,rkn->ran', ham_rows, gathered)

    result = lax.map(one_group, jnp.arange(group_total, dtype=jnp.int32))
    return result.reshape(NB, B, K)


def reference(hamiltonian, column_blocks, block_counts, trial_vectors, spectral_bounds):
    centre = (spectral_bounds[0] + spectral_bounds[1]) / 2.0
    half_width = (spectral_bounds[1] - spectral_bounds[0]) / 2.0
    start_field = trial_vectors.astype(jnp.float32)
    product = apply_blocks(trial_vectors, hamiltonian, column_blocks, block_counts)
    once_filtered = ((product - centre * start_field) / half_width).astype(jnp.bfloat16)
    product = apply_blocks(once_filtered, hamiltonian, column_blocks, block_counts)
    filtered = 2.0 * (product - centre * once_filtered.astype(jnp.float32)) / half_width - start_field
    return filtered.astype(jnp.bfloat16)
```

```python
import jax
import jax.numpy as jnp
from jax import lax
from jax.experimental import pallas as pl
from jax.experimental.pallas import tpu as pltpu
from jax.sharding import PartitionSpec as P

REACH = 16
HALF = REACH // 2
CH = 4


def kernel(idx_ref, bounds_ref, h_hbm, tv_hbm, out_ref, hv, win1, win2,
           rl1, rh1, rl2, rh2, h_sem, tv_sem, send_sem, recv_sem):
    rows = h_hbm.shape[0]
    slots = idx_ref.shape[0]
    window = rows + 2 * REACH
    lo_end, hi_start = REACH, rows - REACH
    n = lax.axis_size("rows")
    me = lax.axis_index("rows")
    right, left = lax.rem(me + 1, n), lax.rem(me + n - 1, n)

    order = (list(range(lo_end, hi_start, CH))
             + list(range(HALF, lo_end, CH)) + list(range(hi_start, hi_start + HALF, CH))
             + list(range(0, HALF, CH)) + list(range(hi_start + HALF, rows, CH)))

    def h_copy(chunk):
        return pltpu.make_async_copy(
            h_hbm.at[pl.ds(chunk * CH, CH)], hv.at[pl.ds(chunk * CH, CH)], h_sem.at[chunk])

    tv_copy = pltpu.make_async_copy(tv_hbm, win1.at[pl.ds(REACH, rows)], tv_sem)
    tv_copy.start()
    for row in order[:2]:
        h_copy(row // CH).start()

    barrier = pltpu.get_barrier_semaphore()
    for neighbour in (left, right):
        pl.semaphore_signal(barrier, inc=1, device_id={"rows": neighbour},
                            device_id_type=pl.DeviceIdType.MESH)
    for row in order[2:]:
        h_copy(row // CH).start()
    zero = jnp.zeros(win1.shape[1:], win1.dtype)
    win1[window] = zero
    win2[window] = zero
    pl.semaphore_wait(barrier, 2)

    def remote(src, dst, k, target):
        return pltpu.make_async_remote_copy(
            src_ref=src, dst_ref=dst, send_sem=send_sem.at[k], recv_sem=recv_sem.at[k],
            device_id={"rows": target}, device_id_type=pl.DeviceIdType.MESH)

    def halo(src, base, low, high, k):
        return (
            remote(src.at[pl.ds(base + rows - HALF, HALF)], low.at[pl.ds(HALF, HALF)], k, right),
            remote(src.at[pl.ds(base, HALF)], high.at[pl.ds(0, HALF)], k + 1, left),
            remote(src.at[pl.ds(base + hi_start, HALF)], low.at[pl.ds(0, HALF)], k + 2, right),
            remote(src.at[pl.ds(base + HALF, HALF)], high.at[pl.ds(HALF, HALF)], k + 3, left),
        )

    first = halo(tv_hbm, 0, rl1, rh1, 0)
    second = halo(win2, REACH, rl2, rh2, 4)
    for copy in first:
        copy.start()

    centre = (bounds_ref[0] + bounds_ref[1]) * 0.5
    half = (bounds_ref[1] - bounds_ref[0]) * 0.5
    inv = 1.0 / jnp.full((1, win1.shape[2]), half, jnp.float32)

    def product(r, win):
        gathered = jnp.concatenate([win[idx_ref[j, r]] for j in range(slots)], axis=0)
        return jnp.dot(hv[r], gathered, preferred_element_type=jnp.float32)

    def one(r):
        v = win1[REACH + r].astype(jnp.float32)
        win2[REACH + r] = ((product(r, win1) - centre * v) * inv).astype(win2.dtype)

    def two(r):
        v = win2[REACH + r].astype(jnp.float32)
        start = win1[REACH + r].astype(jnp.float32)
        out_ref[r] = (2.0 * (product(r, win2) - centre * v) * inv - start).astype(out_ref.dtype)

    def run_one(low, high):
        def body(c, carry):
            h_copy(c).wait()
            for k in range(CH):
                one(c * CH + k)
            return carry
        lax.fori_loop(low // CH, high // CH, body, 0)

    def run_two(low, high):
        def body(c, carry):
            for k in range(CH):
                two(c * CH + k)
            return carry
        lax.fori_loop(low // CH, high // CH, body, 0)

    tv_copy.wait()
    run_one(lo_end, hi_start)
    first[0].wait_recv()
    win1[pl.ds(HALF, HALF)] = rl1[pl.ds(HALF, HALF)]
    run_one(HALF, lo_end)
    second[3].start()
    first[1].wait_recv()
    win1[pl.ds(REACH + rows, HALF)] = rh1[pl.ds(0, HALF)]
    run_one(hi_start, hi_start + HALF)
    second[2].start()
    first[2].wait_recv()
    win1[pl.ds(0, HALF)] = rl1[pl.ds(0, HALF)]
    run_one(0, HALF)
    second[1].start()
    first[3].wait_recv()
    win1[pl.ds(REACH + rows + HALF, HALF)] = rh1[pl.ds(HALF, HALF)]
    run_one(hi_start + HALF, rows)
    second[0].start()

    run_two(lo_end, hi_start)
    second[3].wait_recv()
    second[1].wait_recv()
    win2[pl.ds(REACH + rows, REACH)] = rh2[...]
    run_two(hi_start, rows)
    second[2].wait_recv()
    second[0].wait_recv()
    win2[pl.ds(0, REACH)] = rl2[...]
    run_two(0, lo_end)
    for copy in first + second:
        copy.wait_send()


def local(hamiltonian, column_blocks, block_counts, trial_vectors, spectral_bounds):
    rows, slots = column_blocks.shape
    orbitals, vectors = trial_vectors.shape[1:]
    window = rows + 2 * REACH
    total = rows * lax.axis_size("rows")
    start = lax.axis_index("rows") * rows - REACH
    index = column_blocks.T - start
    index = jnp.where(index < 0, index + total, index)
    index = jnp.where(index >= total, index - total, index)
    used = jnp.arange(slots, dtype=jnp.int32)[:, None] < block_counts[None, :]
    index = jnp.where(used, index, window)

    dtype = trial_vectors.dtype
    panel = lambda count: pltpu.VMEM((count, orbitals, vectors), dtype)
    return pl.pallas_call(
        kernel,
        out_shape=jax.ShapeDtypeStruct(trial_vectors.shape, dtype),
        in_specs=[
            pl.BlockSpec(memory_space=pltpu.SMEM),
            pl.BlockSpec(memory_space=pltpu.SMEM),
            pl.BlockSpec(memory_space=pltpu.HBM),
            pl.BlockSpec(memory_space=pltpu.HBM),
        ],
        out_specs=pl.BlockSpec(memory_space=pltpu.VMEM),
        scratch_shapes=[
            pltpu.VMEM(hamiltonian.shape, hamiltonian.dtype),
            panel(window + 1), panel(window + 1),
            panel(REACH), panel(REACH), panel(REACH), panel(REACH),
            pltpu.SemaphoreType.DMA((rows // CH,)),
            pltpu.SemaphoreType.DMA,
            pltpu.SemaphoreType.DMA((8,)),
            pltpu.SemaphoreType.DMA((8,)),
        ],
        compiler_params=pltpu.CompilerParams(
            collective_id=0, has_side_effects=True, vmem_limit_bytes=56 * 1024 * 1024),
    )(index, spectral_bounds, hamiltonian, trial_vectors)


def solution(mesh):
    placed = (
        P(("groups", "rows"), None, None),
        P(("groups", "rows"), None),
        P(("groups", "rows")),
        P(("groups", "rows"), None, None),
        P("groups"),
    )
    return jax.shard_map(
        local,
        mesh=mesh,
        in_specs=placed,
        out_specs=P(("groups", "rows"), None, None),
        check_vma=False,
    )
```

```python
import jax
import jax.numpy as jnp
from jax import lax
from jax.experimental import pallas as pl
from jax.experimental.pallas import tpu as pltpu
from jax.sharding import PartitionSpec as P

REACH = 16
CH = REACH // 2
VMEM_LIMIT = 56 * 1024 * 1024


def kernel(columns_hbm, counts_hbm, bounds_hbm, h_hbm, tv_hbm, out_ref,
           columns, counts, table, idx_ref, bounds_ref, hv, win1, win2,
           rl1, rh1, rl2, rh2, small_sem, h_sem, send_sem, recv_sem):
    rows = h_hbm.shape[0]
    slots = columns_hbm.shape[0]
    orbitals, vectors = tv_hbm.shape[1:]
    window = rows + 2 * REACH
    hi_start = rows - REACH
    low_mid, high_mid = REACH // CH, hi_start // CH
    inner = high_mid - low_mid
    chunks = rows // CH
    n = lax.axis_size("rows")
    me = lax.axis_index("rows")
    right, left = lax.rem(me + 1, n), lax.rem(me + n - 1, n)

    barrier = pltpu.get_barrier_semaphore()
    for neighbour in (left, right):
        pl.semaphore_signal(barrier, inc=1, device_id={"rows": neighbour},
                            device_id_type=pl.DeviceIdType.MESH)

    def h_copy(c):
        return pltpu.make_async_copy(
            h_hbm.at[pl.ds(c * CH, CH)], hv.at[pl.ds(c * CH, CH)], h_sem.at[c])

    small = [
        pltpu.make_async_copy(columns_hbm, columns, small_sem.at[0]),
        pltpu.make_async_copy(counts_hbm, counts, small_sem.at[1]),
        pltpu.make_async_copy(bounds_hbm, bounds_ref, small_sem.at[2]),
        pltpu.make_async_copy(tv_hbm, win1.at[pl.ds(REACH, rows)], small_sem.at[3]),
    ]
    table_copy = pltpu.make_async_copy(table, idx_ref, small_sem.at[4])
    for copy in small:
        copy.start()
    for c in ([low_mid + k for k in range(inner)]
              + [c for k in range(low_mid) for c in (low_mid - 1 - k, high_mid + k)]):
        h_copy(c).start()

    def remote(src, dst, k, target):
        return pltpu.make_async_remote_copy(
            src_ref=src, dst_ref=dst, send_sem=send_sem.at[k], recv_sem=recv_sem.at[k],
            device_id={"rows": target}, device_id_type=pl.DeviceIdType.MESH)

    def halo(src, base, low, high, k):
        return (
            remote(src.at[pl.ds(base + rows - CH, CH)], low.at[pl.ds(CH, CH)], k, right),
            remote(src.at[pl.ds(base, CH)], high.at[pl.ds(0, CH)], k + 1, left),
            remote(src.at[pl.ds(base + hi_start, CH)], low.at[pl.ds(0, CH)], k + 2, right),
            remote(src.at[pl.ds(base + CH, CH)], high.at[pl.ds(CH, CH)], k + 3, left),
        )

    first = halo(tv_hbm, 0, rl1, rh1, 0)
    second = halo(win2, REACH, rl2, rh2, 4)
    pl.semaphore_wait(barrier, 2)
    for copy in first:
        copy.start()

    small[0].wait()
    small[1].wait()
    total = rows * n
    index = columns[...] - (me * rows - REACH)
    index = jnp.where(index < 0, index + total, index)
    index = jnp.where(index >= total, index - total, index)
    used = lax.broadcasted_iota(jnp.int32, index.shape, 0) < counts[...]
    table[...] = jnp.where(used, index, window)
    table_copy.start()

    zero = jnp.zeros(win1.shape[1:], win1.dtype)
    win1[window] = zero
    win2[window] = zero
    small[2].wait()
    centre = (bounds_ref[0] + bounds_ref[1]) * 0.5
    half = (bounds_ref[1] - bounds_ref[0]) * 0.5
    inv = 1.0 / jnp.full((1, vectors), half, jnp.float32)

    def products(r, win):
        gathered = jnp.concatenate(
            [jnp.concatenate([win[idx_ref[j, r]], win[idx_ref[j, r + 1]]], axis=1)
             for j in range(slots)], axis=0)
        both = jnp.dot(jnp.concatenate([hv[r], hv[r + 1]], axis=0), gathered,
                       preferred_element_type=jnp.float32)
        return both[:orbitals, :vectors], both[orbitals:, vectors:]

    def one(c):
        for k in range(0, CH, 2):
            r = c * CH + k
            for q, product in enumerate(products(r, win1)):
                v = win1[REACH + r + q].astype(jnp.float32)
                win2[REACH + r + q] = ((product - centre * v) * inv).astype(win2.dtype)

    def two(c):
        for k in range(0, CH, 2):
            r = c * CH + k
            for q, product in enumerate(products(r, win2)):
                v = win2[REACH + r + q].astype(jnp.float32)
                start = win1[REACH + r + q].astype(jnp.float32)
                out_ref[r + q] = (2.0 * (product - centre * v) * inv - start).astype(out_ref.dtype)

    def step_one(i, carry):
        k = i - inner
        edge = jnp.where(lax.rem(k, 2) == 0, low_mid - 1 - k // 2, high_mid + k // 2)
        c = jnp.where(i < inner, low_mid + i, edge)

        @pl.when(i == inner)
        def _():
            first[0].wait_recv()
            win1[pl.ds(CH, CH)] = rl1[pl.ds(CH, CH)]

        @pl.when(i == inner + 1)
        def _():
            first[1].wait_recv()
            win1[pl.ds(REACH + rows, CH)] = rh1[pl.ds(0, CH)]

        @pl.when(i == inner + 2)
        def _():
            first[2].wait_recv()
            win1[pl.ds(0, CH)] = rl1[pl.ds(0, CH)]

        @pl.when(i == inner + 3)
        def _():
            first[3].wait_recv()
            win1[pl.ds(REACH + rows + CH, CH)] = rh1[pl.ds(CH, CH)]

        h_copy(c).wait()
        one(c)
        for at, copy in ((0, second[3]), (1, second[2]), (2, second[1]), (3, second[0])):
            @pl.when(i == inner + at)
            def _():
                copy.start()
        return carry

    def step_two(i, carry):
        c = jnp.where(i < chunks - low_mid, low_mid + i, chunks - 1 - i)

        @pl.when(i == inner)
        def _():
            second[1].wait_recv()
            win2[pl.ds(REACH + rows, CH)] = rh2[pl.ds(0, CH)]

        @pl.when(i == inner + 1)
        def _():
            second[3].wait_recv()
            win2[pl.ds(REACH + rows + CH, CH)] = rh2[pl.ds(CH, CH)]

        @pl.when(i == inner + 2)
        def _():
            second[0].wait_recv()
            win2[pl.ds(CH, CH)] = rl2[pl.ds(CH, CH)]

        @pl.when(i == inner + 3)
        def _():
            second[2].wait_recv()
            win2[pl.ds(0, CH)] = rl2[pl.ds(0, CH)]

        two(c)
        return carry

    small[3].wait()
    table_copy.wait()
    lax.fori_loop(0, chunks, step_one, 0)
    lax.fori_loop(0, chunks, step_two, 0)
    for copy in first + second:
        copy.wait_send()


def local(hamiltonian, column_blocks, block_counts, trial_vectors, spectral_bounds):
    rows, slots = column_blocks.shape
    orbitals, vectors = trial_vectors.shape[1:]
    window = rows + 2 * REACH
    dtype = trial_vectors.dtype
    panel = lambda count: pltpu.VMEM((count, orbitals, vectors), dtype)
    return pl.pallas_call(
        kernel,
        out_shape=jax.ShapeDtypeStruct(trial_vectors.shape, dtype),
        in_specs=[pl.BlockSpec(memory_space=pl.ANY)] * 5,
        out_specs=pl.BlockSpec(memory_space=pltpu.VMEM),
        scratch_shapes=[
            pltpu.VMEM((slots, rows), jnp.int32),
            pltpu.VMEM((1, rows), jnp.int32),
            pltpu.VMEM((slots, rows), jnp.int32),
            pltpu.SMEM((slots, rows), jnp.int32),
            pltpu.SMEM(spectral_bounds.shape, spectral_bounds.dtype),
            pltpu.VMEM(hamiltonian.shape, hamiltonian.dtype),
            panel(window + 1), panel(window + 1),
            panel(REACH), panel(REACH), panel(REACH), panel(REACH),
            pltpu.SemaphoreType.DMA((5,)),
            pltpu.SemaphoreType.DMA((rows // CH,)),
            pltpu.SemaphoreType.DMA((8,)),
            pltpu.SemaphoreType.DMA((8,)),
        ],
        compiler_params=pltpu.CompilerParams(
            collective_id=0, has_side_effects=True, vmem_limit_bytes=VMEM_LIMIT),
    )(column_blocks.T, block_counts.reshape(1, rows), spectral_bounds, hamiltonian, trial_vectors)


def solution(mesh):
    placed = (
        P(("groups", "rows"), None, None),
        P(("groups", "rows"), None),
        P(("groups", "rows")),
        P(("groups", "rows"), None, None),
        P("groups"),
    )
    return jax.shard_map(
        local,
        mesh=mesh,
        in_specs=placed,
        out_specs=P(("groups", "rows"), None, None),
        check_vma=False,
    )
```

```python
import jax
import jax.numpy as jnp
from jax import lax
from jax.experimental import pallas as pl
from jax.experimental.pallas import tpu as pltpu
from jax.sharding import PartitionSpec as P

REACH = 16
CH = REACH // 2
VMEM_LIMIT = 56 * 1024 * 1024


def kernel(columns_hbm, counts_hbm, bounds_hbm, h_hbm, tv_hbm, out_hbm,
           columns, counts, table, idx_ref, bounds_ref, hv, win1, win2, out_ref,
           rl1, rh1, rl2, rh2, small_sem, h_sem, out_sem, send_sem, recv_sem):
    rows = h_hbm.shape[0]
    slots = columns_hbm.shape[0]
    orbitals, vectors = tv_hbm.shape[1:]
    window = rows + 2 * REACH
    hi_start = rows - REACH
    low_mid, high_mid = REACH // CH, hi_start // CH
    inner = high_mid - low_mid
    chunks = rows // CH
    n = lax.axis_size("rows")
    me = lax.axis_index("rows")
    right, left = lax.rem(me + 1, n), lax.rem(me + n - 1, n)

    barrier = pltpu.get_barrier_semaphore()
    for neighbour in (left, right):
        pl.semaphore_signal(barrier, inc=1, device_id={"rows": neighbour},
                            device_id_type=pl.DeviceIdType.MESH)

    def h_copy(c):
        return pltpu.make_async_copy(
            h_hbm.at[pl.ds(c * CH, CH)], hv.at[pl.ds(c * CH, CH)], h_sem.at[c])

    def out_copy(c):
        return pltpu.make_async_copy(
            out_ref.at[pl.ds(c * CH, CH)], out_hbm.at[pl.ds(c * CH, CH)], out_sem.at[c])

    small = [
        pltpu.make_async_copy(columns_hbm, columns, small_sem.at[0]),
        pltpu.make_async_copy(counts_hbm, counts, small_sem.at[1]),
        pltpu.make_async_copy(bounds_hbm, bounds_ref, small_sem.at[2]),
        pltpu.make_async_copy(tv_hbm, win1.at[pl.ds(REACH, rows)], small_sem.at[3]),
    ]
    table_copy = pltpu.make_async_copy(table, idx_ref, small_sem.at[4])
    for copy in small:
        copy.start()
    for c in ([low_mid + k for k in range(inner)]
              + [c for k in range(low_mid) for c in (low_mid - 1 - k, high_mid + k)]):
        h_copy(c).start()

    def remote(src, dst, k, target):
        return pltpu.make_async_remote_copy(
            src_ref=src, dst_ref=dst, send_sem=send_sem.at[k], recv_sem=recv_sem.at[k],
            device_id={"rows": target}, device_id_type=pl.DeviceIdType.MESH)

    def halo(src, base, low, high, k):
        return (
            remote(src.at[pl.ds(base + rows - CH, CH)], low.at[pl.ds(CH, CH)], k, right),
            remote(src.at[pl.ds(base, CH)], high.at[pl.ds(0, CH)], k + 1, left),
            remote(src.at[pl.ds(base + hi_start, CH)], low.at[pl.ds(0, CH)], k + 2, right),
            remote(src.at[pl.ds(base + CH, CH)], high.at[pl.ds(CH, CH)], k + 3, left),
        )

    first = halo(tv_hbm, 0, rl1, rh1, 0)
    second = halo(win2, REACH, rl2, rh2, 4)
    pl.semaphore_wait(barrier, 2)
    for copy in first:
        copy.start()

    small[0].wait()
    small[1].wait()
    total = rows * n
    index = columns[...] - (me * rows - REACH)
    index = jnp.where(index < 0, index + total, index)
    index = jnp.where(index >= total, index - total, index)
    used = lax.broadcasted_iota(jnp.int32, index.shape, 0) < counts[...]
    table[...] = jnp.where(used, index, window)
    table_copy.start()

    zero = jnp.zeros(win1.shape[1:], win1.dtype)
    win1[window] = zero
    win2[window] = zero
    small[2].wait()
    centre = (bounds_ref[0] + bounds_ref[1]) * 0.5
    half = (bounds_ref[1] - bounds_ref[0]) * 0.5
    inv = 1.0 / jnp.full((1, vectors), half, jnp.float32)

    def products(r, win):
        gathered = jnp.concatenate(
            [jnp.concatenate([win[idx_ref[j, r]], win[idx_ref[j, r + 1]]], axis=1)
             for j in range(slots)], axis=0)
        both = jnp.dot(jnp.concatenate([hv[r], hv[r + 1]], axis=0), gathered,
                       preferred_element_type=jnp.float32)
        return both[:orbitals, :vectors], both[orbitals:, vectors:]

    def one(c):
        for k in range(0, CH, 2):
            r = c * CH + k
            for q, product in enumerate(products(r, win1)):
                v = win1[REACH + r + q].astype(jnp.float32)
                win2[REACH + r + q] = ((product - centre * v) * inv).astype(win2.dtype)

    def two(c):
        for k in range(0, CH, 2):
            r = c * CH + k
            for q, product in enumerate(products(r, win2)):
                v = win2[REACH + r + q].astype(jnp.float32)
                start = win1[REACH + r + q].astype(jnp.float32)
                out_ref[r + q] = (2.0 * (product - centre * v) * inv - start).astype(out_ref.dtype)

    odd = lax.rem(me, 2)

    def edge_chunk(e):
        far = e // 2
        return jnp.where(lax.rem(e, 2) == 0, low_mid - 1 - far, high_mid + far)

    def swap_sides(e):
        return jnp.where(odd == 1, e + 1 - 2 * lax.rem(e, 2), e)

    def step_one(i, carry):
        p = jnp.maximum(i - inner, 0)
        e = swap_sides(jnp.where(p < 2, p, 5 - p))
        c = jnp.where(i < inner, low_mid + i, edge_chunk(e))
        halo_parts = ((0, rl1, CH, CH), (1, rh1, 0, REACH + rows),
                      (2, rl1, 0, 0), (3, rh1, CH, REACH + rows + CH))
        for at, source, base, target in halo_parts:
            @pl.when(jnp.logical_and(i >= inner, e == at))
            def _():
                first[at].wait_recv()
                win1[pl.ds(target, CH)] = source[pl.ds(base, CH)]

        h_copy(c).wait()
        one(c)
        for at in range(4):
            @pl.when(jnp.logical_and(i >= inner, e == at))
            def _():
                second[3 - at].start()
        return carry

    def step_two(i, carry):
        p = jnp.maximum(i - inner, 0)
        e = swap_sides(1 - p // 2 + 2 * lax.rem(p, 2))
        c = jnp.where(i < inner, low_mid + i, edge_chunk(e))
        halo_parts = ((0, rl2, CH, CH), (1, rh2, 0, REACH + rows),
                      (2, rl2, 0, 0), (3, rh2, CH, REACH + rows + CH))
        for at, source, base, target in halo_parts:
            @pl.when(jnp.logical_and(i >= inner, e == at))
            def _():
                second[at].wait_recv()
                win2[pl.ds(target, CH)] = source[pl.ds(base, CH)]

        two(c)
        out_copy(c).start()
        return carry

    small[3].wait()
    table_copy.wait()
    lax.fori_loop(0, chunks, step_one, 0)
    lax.fori_loop(0, chunks, step_two, 0)
    for copy in first + second:
        copy.wait_send()
    for c in range(chunks):
        out_copy(c).wait()


def local(hamiltonian, column_blocks, block_counts, trial_vectors, spectral_bounds):
    rows, slots = column_blocks.shape
    orbitals, vectors = trial_vectors.shape[1:]
    window = rows + 2 * REACH
    dtype = trial_vectors.dtype
    panel = lambda count: pltpu.VMEM((count, orbitals, vectors), dtype)
    return pl.pallas_call(
        kernel,
        out_shape=jax.ShapeDtypeStruct(trial_vectors.shape, dtype),
        in_specs=[pl.BlockSpec(memory_space=pl.ANY)] * 5,
        out_specs=pl.BlockSpec(memory_space=pl.ANY),
        scratch_shapes=[
            pltpu.VMEM((slots, rows), jnp.int32),
            pltpu.VMEM((1, rows), jnp.int32),
            pltpu.VMEM((slots, rows), jnp.int32),
            pltpu.SMEM((slots, rows), jnp.int32),
            pltpu.SMEM(spectral_bounds.shape, spectral_bounds.dtype),
            pltpu.VMEM(hamiltonian.shape, hamiltonian.dtype),
            panel(window + 1), panel(window + 1), panel(rows),
            panel(REACH), panel(REACH), panel(REACH), panel(REACH),
            pltpu.SemaphoreType.DMA((5,)),
            pltpu.SemaphoreType.DMA((rows // CH,)),
            pltpu.SemaphoreType.DMA((rows // CH,)),
            pltpu.SemaphoreType.DMA((8,)),
            pltpu.SemaphoreType.DMA((8,)),
        ],
        compiler_params=pltpu.CompilerParams(
            collective_id=0, has_side_effects=True, vmem_limit_bytes=VMEM_LIMIT),
    )(column_blocks.T, block_counts.reshape(1, rows), spectral_bounds, hamiltonian, trial_vectors)


def solution(mesh):
    placed = (
        P(("groups", "rows"), None, None),
        P(("groups", "rows"), None),
        P(("groups", "rows")),
        P(("groups", "rows"), None, None),
        P("groups"),
    )
    return jax.shard_map(
        local,
        mesh=mesh,
        in_specs=placed,
        out_specs=P(("groups", "rows"), None, None),
        check_vma=False,
    )
```

```python
import jax
import jax.numpy as jnp
from jax import lax
from jax.experimental import pallas as pl
from jax.experimental.pallas import tpu as pltpu
from jax.sharding import PartitionSpec as P

REACH = 16
CH = REACH // 2
VMEM_LIMIT = 56 * 1024 * 1024


def kernel(columns_hbm, counts_hbm, bounds_hbm, h_hbm, tv_hbm, out_hbm,
           columns, counts, table, idx_ref, bounds_ref, hv, win1, win2, out_ref,
           rl1, rh1, rl2, rh2, small_sem, h_sem, out_sem, send_sem, recv_sem):
    rows = h_hbm.shape[0]
    slots = columns_hbm.shape[0]
    orbitals, vectors = tv_hbm.shape[1:]
    window = rows + 2 * REACH
    hi_start = rows - REACH
    low_mid, high_mid = REACH // CH, hi_start // CH
    inner = high_mid - low_mid
    chunks = rows // CH
    n = lax.axis_size("rows")
    me = lax.axis_index("rows")
    right, left = lax.rem(me + 1, n), lax.rem(me + n - 1, n)

    barrier = pltpu.get_barrier_semaphore()
    for neighbour in (left, right):
        pl.semaphore_signal(barrier, inc=1, device_id={"rows": neighbour},
                            device_id_type=pl.DeviceIdType.MESH)

    def h_copy(c):
        return pltpu.make_async_copy(
            h_hbm.at[pl.ds(c * CH, CH)], hv.at[pl.ds(c * CH, CH)], h_sem.at[c])

    def out_copy(c):
        return pltpu.make_async_copy(
            out_ref.at[pl.ds(c * CH, CH)], out_hbm.at[pl.ds(c * CH, CH)], out_sem.at[c])

    small = [
        pltpu.make_async_copy(columns_hbm, columns, small_sem.at[0]),
        pltpu.make_async_copy(counts_hbm, counts, small_sem.at[1]),
        pltpu.make_async_copy(bounds_hbm, bounds_ref, small_sem.at[2]),
        pltpu.make_async_copy(tv_hbm, win1.at[pl.ds(REACH, rows)], small_sem.at[3]),
    ]
    table_copy = pltpu.make_async_copy(table, idx_ref, small_sem.at[4])
    for copy in small:
        copy.start()
    for c in ([low_mid + k for k in range(inner)]
              + [c for k in range(low_mid) for c in (low_mid - 1 - k, high_mid + k)]):
        h_copy(c).start()

    def remote(src, dst, k, target):
        return pltpu.make_async_remote_copy(
            src_ref=src, dst_ref=dst, send_sem=send_sem.at[k], recv_sem=recv_sem.at[k],
            device_id={"rows": target}, device_id_type=pl.DeviceIdType.MESH)

    def halo(src, base, low, high, k):
        return (
            remote(src.at[pl.ds(base + rows - CH, CH)], low.at[pl.ds(CH, CH)], k, right),
            remote(src.at[pl.ds(base, CH)], high.at[pl.ds(0, CH)], k + 1, left),
            remote(src.at[pl.ds(base + hi_start, CH)], low.at[pl.ds(0, CH)], k + 2, right),
            remote(src.at[pl.ds(base + CH, CH)], high.at[pl.ds(CH, CH)], k + 3, left),
        )

    first = halo(tv_hbm, 0, rl1, rh1, 0)
    second = halo(win2, REACH, rl2, rh2, 4)
    pl.semaphore_wait(barrier, 2)
    for copy in first:
        copy.start()

    small[0].wait()
    small[1].wait()
    total = rows * n
    index = columns[...] - (me * rows - REACH)
    index = jnp.where(index < 0, index + total, index)
    index = jnp.where(index >= total, index - total, index)
    used = lax.broadcasted_iota(jnp.int32, index.shape, 0) < counts[...]
    table[...] = jnp.where(used, index, window)
    table_copy.start()

    zero = jnp.zeros(win1.shape[1:], win1.dtype)
    win1[window] = zero
    win2[window] = zero
    small[2].wait()
    centre = (bounds_ref[0] + bounds_ref[1]) * 0.5
    half = (bounds_ref[1] - bounds_ref[0]) * 0.5
    inv = 1.0 / jnp.full((1, vectors), half, jnp.float32)

    def products(r, win):
        gathered = jnp.concatenate(
            [jnp.concatenate([win[idx_ref[j, r]], win[idx_ref[j, r + 1]]], axis=1)
             for j in range(slots)], axis=0)
        both = jnp.dot(jnp.concatenate([hv[r], hv[r + 1]], axis=0), gathered,
                       preferred_element_type=jnp.float32)
        return both[:orbitals, :vectors], both[orbitals:, vectors:]

    def one(c):
        for k in range(0, CH, 2):
            r = c * CH + k
            for q, product in enumerate(products(r, win1)):
                v = win1[REACH + r + q].astype(jnp.float32)
                win2[REACH + r + q] = ((product - centre * v) * inv).astype(win2.dtype)

    def two(c):
        for k in range(0, CH, 2):
            r = c * CH + k
            for q, product in enumerate(products(r, win2)):
                v = win2[REACH + r + q].astype(jnp.float32)
                start = win1[REACH + r + q].astype(jnp.float32)
                out_ref[r + q] = (2.0 * (product - centre * v) * inv - start).astype(out_ref.dtype)

    odd = lax.rem(me, 2)

    def edge_chunk(e):
        far = e // 2
        return jnp.where(lax.rem(e, 2) == 0, low_mid - 1 - far, high_mid + far)

    def swap_sides(e):
        return jnp.where(odd == 1, e + 1 - 2 * lax.rem(e, 2), e)

    def step_one(i, carry):
        p = jnp.maximum(i - inner, 0)
        e = swap_sides(1 - p // 2 + 2 * lax.rem(p, 2))
        c = jnp.where(i < inner, low_mid + i, edge_chunk(e))
        halo_parts = ((0, rl1, CH, CH), (1, rh1, 0, REACH + rows),
                      (2, rl1, 0, 0), (3, rh1, CH, REACH + rows + CH))
        for at, source, base, target in halo_parts:
            @pl.when(jnp.logical_and(i >= inner, e == at))
            def _():
                first[at].wait_recv()
                win1[pl.ds(target, CH)] = source[pl.ds(base, CH)]

        h_copy(c).wait()
        one(c)
        for at in range(4):
            @pl.when(jnp.logical_and(i >= inner, e == at))
            def _():
                second[3 - at].start()
        return carry

    def step_two(i, carry):
        p = jnp.maximum(i - inner, 0)
        e = swap_sides(1 - p // 2 + 2 * lax.rem(p, 2))
        c = jnp.where(i < inner, low_mid + i, edge_chunk(e))
        halo_parts = ((0, rl2, CH, CH), (1, rh2, 0, REACH + rows),
                      (2, rl2, 0, 0), (3, rh2, CH, REACH + rows + CH))
        for at, source, base, target in halo_parts:
            @pl.when(jnp.logical_and(i >= inner, e == at))
            def _():
                second[at].wait_recv()
                win2[pl.ds(target, CH)] = source[pl.ds(base, CH)]

        two(c)
        out_copy(c).start()
        return carry

    small[3].wait()
    table_copy.wait()
    lax.fori_loop(0, chunks, step_one, 0)
    lax.fori_loop(0, chunks, step_two, 0)
    for copy in first + second:
        copy.wait_send()
    for c in range(chunks):
        out_copy(c).wait()


def local(hamiltonian, column_blocks, block_counts, trial_vectors, spectral_bounds):
    rows, slots = column_blocks.shape
    orbitals, vectors = trial_vectors.shape[1:]
    window = rows + 2 * REACH
    dtype = trial_vectors.dtype
    panel = lambda count: pltpu.VMEM((count, orbitals, vectors), dtype)
    return pl.pallas_call(
        kernel,
        out_shape=jax.ShapeDtypeStruct(trial_vectors.shape, dtype),
        in_specs=[pl.BlockSpec(memory_space=pl.ANY)] * 5,
        out_specs=pl.BlockSpec(memory_space=pl.ANY),
        scratch_shapes=[
            pltpu.VMEM((slots, rows), jnp.int32),
            pltpu.VMEM((1, rows), jnp.int32),
            pltpu.VMEM((slots, rows), jnp.int32),
            pltpu.SMEM((slots, rows), jnp.int32),
            pltpu.SMEM(spectral_bounds.shape, spectral_bounds.dtype),
            pltpu.VMEM(hamiltonian.shape, hamiltonian.dtype),
            panel(window + 1), panel(window + 1), panel(rows),
            panel(REACH), panel(REACH), panel(REACH), panel(REACH),
            pltpu.SemaphoreType.DMA((5,)),
            pltpu.SemaphoreType.DMA((rows // CH,)),
            pltpu.SemaphoreType.DMA((rows // CH,)),
            pltpu.SemaphoreType.DMA((8,)),
            pltpu.SemaphoreType.DMA((8,)),
        ],
        compiler_params=pltpu.CompilerParams(
            collective_id=0, has_side_effects=True, vmem_limit_bytes=VMEM_LIMIT),
    )(column_blocks.T, block_counts.reshape(1, rows), spectral_bounds, hamiltonian, trial_vectors)


def solution(mesh):
    placed = (
        P(("groups", "rows"), None, None),
        P(("groups", "rows"), None),
        P(("groups", "rows")),
        P(("groups", "rows"), None, None),
        P("groups"),
    )
    return jax.shard_map(
        local,
        mesh=mesh,
        in_specs=placed,
        out_specs=P(("groups", "rows"), None, None),
        check_vma=False,
    )
```
